32 devices in a mesh: tiles: 2 (over x), date: 8 (over z, y), row: 2 (over core).
Axes of the slice: x: 2, y: 2, z: 4, core: 2. Of those that a mesh axis runs over, the one named last changes fastest.
Arguments:
- slc_stack: bfloat16 [16, 2, 256, 1024], P('date', None, ('tiles', 'row')), parts along dimension 2, as said below
- partners: int32 [16, 4], P('date'), may hold values from 0 to 15, as said below
- counts: int32 [16], P('date'), may hold values from 1 to 4, as said below
- windows: int32 [16, 4], P('date'), may hold values from 3 to 5
Outputs:
- coherence: bfloat16 [16, 4, 256, 1024], P('date', None, ('tiles', 'row')), parts along dimension 2
The draws below stay inside these ranges and needn't reach their ends.
There are 2 independent parts, one for each index of `tiles`. The reference program is written for one: setup_inputs(seed, part) draws one part's arguments, and reference() takes and returns one part's arrays. A program takes and returns all parts, laid end to end along the dimension named above; an argument that names none is the same for every part. Nothing has to cross between parts.
Inputs may be any that keep to these rules, and one draw needn't show every extreme that they name: The partners of date d are (d + o) mod 16 for distinct offsets o from 1 to 4; some date has a first partner exactly 4 ahead. `counts`: of the 2 dates held by one device along `date`, at most one has more than 2 pairs, so those dates have 6 pairs or fewer together; some device's pair of dates has exactly 6, and some date has 4. `slc_stack`: every pixel's magnitude is 0.5 or more.
All inputs are finite; a program needn't handle non-finite values.
Results may differ from the reference program's by a relative error of at most 0.001.
Values may be sent and summed in bfloat16 or wider, within the bound.
A program may use at most 64 MiB of HBM per device.

```python
import math
import jax
import jax.numpy as jnp
from jax import lax

DATES_DEV = 2
COLS = 1024
MAXOFF = 4
MAXP = 4
HALF = 2
NDATES = 16
ROWS = 128


def draw_slc_stack(key, part):
    keys = jax.random.split(key, 4)
    base_phase = jax.random.uniform(keys[0], (1, ROWS, COLS), jnp.float32, -math.pi, math.pi)
    spread = jnp.exp(jax.random.uniform(keys[1], (NDATES, 1, 1), jnp.float32, math.log(0.2), math.log(2.5)))
    amplitude = jnp.exp(jax.random.uniform(keys[2], (NDATES, ROWS, COLS), jnp.float32, math.log(0.5), math.log(4.0)))
    noise = jax.random.normal(keys[3], (NDATES, ROWS, COLS), jnp.float32)
    phase = base_phase + spread * noise
    real_part = amplitude * jnp.cos(phase)
    imag_part = amplitude * jnp.sin(phase)
    return jnp.stack([real_part, imag_part], axis=1).astype(jnp.bfloat16)


def draw_partners(key, part):
    scores = jax.random.randint(key, (NDATES, MAXOFF), 0, 1 << 20) * MAXOFF + jnp.arange(MAXOFF, dtype=jnp.int32)[None, :]
    offsets = jnp.argsort(scores, axis=1, stable=True).astype(jnp.int32) + 1
    far_place = jnp.argmax(offsets == MAXOFF, axis=1).astype(jnp.int32)
    column_ids = jnp.arange(MAXOFF, dtype=jnp.int32)[None, :]
    swapped = jnp.where(column_ids == 0, MAXOFF, jnp.where(column_ids == far_place[:, None], offsets[:, 0:1], offsets))
    date_ids = jnp.arange(NDATES, dtype=jnp.int32)[:, None]
    forced = jnp.logical_or(date_ids == NDATES - MAXOFF, date_ids == NDATES - 1 - MAXOFF)
    offsets = jnp.where(forced, swapped, offsets)
    return ((date_ids + offsets[:, 0:MAXP]) % NDATES).astype(jnp.int32)


def draw_counts(key, part):
    groups = NDATES // DATES_DEV
    keys = [jax.random.fold_in(key, 21 + number) for number in range(4)]
    base_counts = jax.random.randint(keys[0], (groups, DATES_DEV), 1, HALF + 1)
    heavy_place = jax.random.randint(keys[1], (groups, 1), 0, DATES_DEV)
    heavy_count = jax.random.randint(keys[2], (groups, 1), 1, MAXP + 1)
    column_ids = jnp.arange(DATES_DEV, dtype=jnp.int32)[None, :]
    result = jnp.where(column_ids == heavy_place, heavy_count, base_counts)
    full_group = jax.random.randint(keys[3], (), 0, groups)
    forced = jnp.where(column_ids == heavy_place, MAXP, HALF)
    group_ids = jnp.arange(groups, dtype=jnp.int32)[:, None]
    result = jnp.where(group_ids == full_group, forced, result)
    return result.reshape(NDATES).astype(jnp.int32)


def place_ends(entries, own_key, low, largest):
    index_at = [jax.random.randint(jax.random.fold_in(own_key, axis), (), 0, length) for axis, length in enumerate(entries.shape)]
    main_axis = entries.shape.index(max(entries.shape))
    neighbour = index_at[:main_axis] + [(index_at[main_axis] + 1) % entries.shape[main_axis]] + index_at[main_axis + 1:]
    return entries.at[tuple(index_at)].set(low).at[tuple(neighbour)].set(largest)


def setup_inputs(seed: int = 0, part: int = 0) -> dict:
    seeds = jax.random.split(jax.random.key(seed), 5)
    part_keys = jax.random.split(jax.random.fold_in(seeds[4], part), 5)
    return {
        "slc_stack": draw_slc_stack(jax.random.fold_in(jax.random.fold_in(seeds[4], part), 71), part),
        "partners": draw_partners(jax.random.fold_in(seeds[4], 71), part),
        "counts": draw_counts(jax.random.fold_in(seeds[4], 71), part),
        "windows": place_ends(jax.random.randint(seeds[3], (NDATES, MAXP), 3, 6), jax.random.fold_in(seeds[3], 1), 3, 5).astype(jnp.int32),
    }


def pair_products(first_block, second_block):
    first_re = first_block[0].astype(jnp.float32)
    first_im = first_block[1].astype(jnp.float32)
    second_re = second_block[0].astype(jnp.float32)
    second_im = second_block[1].astype(jnp.float32)
    cross_re = first_re * second_re + first_im * second_im
    cross_im = first_im * second_re - first_re * second_im
    power_first = first_re * first_re + first_im * first_im
    power_second = second_re * second_re + second_im * second_im
    return jnp.stack([cross_re, cross_im, power_first, power_second])

def range_boxcar(stacked, half_width):
    columns = stacked.shape[-1]
    padded = jnp.pad(stacked, ((0, 0), (0, 0), (5, 5)))
    summed = jnp.zeros_like(stacked)
    for offset in range(-5, 6):
        weight = jnp.where(half_width >= abs(offset), 1.0, 0.0).astype(jnp.float32)
        summed = summed + weight * padded[:, :, 5 + offset:5 + offset + columns]
    return summed

def row_boxcar(extended, strip_rows):
    summed = extended[:, 0:strip_rows, :]
    for offset in range(1, 5):
        summed = summed + extended[:, offset:offset + strip_rows, :]
    return summed

def coherence_of(sums):
    magnitude = jnp.sqrt(sums[0] * sums[0] + sums[1] * sums[1])
    return magnitude / jnp.sqrt(sums[2] * sums[3])

def reference(slc_stack, partners, counts, windows):
    total_dates = slc_stack.shape[0]
    per_date = partners.shape[1]
    slot_total = total_dates * per_date

    def one_pair(slot_id):
        own_date = slot_id // per_date
        slot_index = slot_id % per_date
        partner_date = partners[own_date, slot_index]
        half_width = windows[own_date, slot_index]
        stacked = pair_products(slc_stack[own_date], slc_stack[partner_date])
        summed = range_boxcar(stacked, half_width)
        padded = jnp.pad(summed, ((0, 0), (2, 2), (0, 0)))
        sums = row_boxcar(padded, summed.shape[1])
        result = coherence_of(sums)
        return jnp.where(slot_index < counts[own_date], result, 0.0).astype(jnp.bfloat16)
    blocks = lax.map(one_pair, jnp.arange(slot_total, dtype=jnp.int32))
    return blocks.reshape(total_dates, per_date, slc_stack.shape[2], slc_stack.shape[3])
```

```python
import functools
import jax
import jax.numpy as jnp
from jax import lax
from jax.experimental import pallas as pl
from jax.experimental.pallas import tpu as pltpu
from jax.sharding import PartitionSpec as P

MESH = pl.DeviceIdType.MESH
LANES = 128
PIECE = 32


def exchange_kernel(loop_size, reach, slc_ref, got_ref, edge_ref, pack, *sems):
    direct_send, direct_recv, near_send, near_recv, edge_send, edge_recv = sems
    dates, parts, rows, columns = slc_ref.shape
    tile = lax.axis_index("tiles")
    me = lax.axis_index("date")
    row = lax.axis_index("row")
    pieces = [
        (d, c, pl.ds(r, PIECE)) for d in range(dates) for c in range(parts) for r in range(0, rows, PIECE)
    ]
    relayed = reach == 2

    def at(steps, other=False):
        there = lax.rem(me + steps + loop_size, loop_size)
        return (tile, there, 1 - row if other else row)

    barrier = pltpu.get_barrier_semaphore()

    def greet(device):
        pl.semaphore_signal(barrier, inc=1, device_id=device, device_id_type=MESH)

    even = lax.rem(me, 2) == 0
    for k in range(reach + 1):
        greet(at(k, other=True))
    if relayed:
        greet(at(2))
        greet(at(jnp.where(even, 1, -1)))
    else:
        for k in range(1, reach + 1):
            greet(at(k))

    picked = []
    for d in range(dates):
        for c in range(parts):
            last = slc_ref[d, c, rows - 16 : rows, :].astype(jnp.float32)[14:16]
            first = slc_ref[d, c, 0:16, :].astype(jnp.float32)[0:2]
            picked.append(jnp.where(row == 0, last, first))
    spare = pack.shape[0] - 2 * len(picked)
    if spare:
        picked.append(jnp.zeros((spare, columns), jnp.float32))
    pack[...] = jnp.concatenate(picked, axis=0).astype(jnp.bfloat16)

    pl.semaphore_wait(barrier, 2 * reach + 1)

    def far(k, n):
        d, c, r = pieces[n]
        return pltpu.make_async_remote_copy(
            src_ref=slc_ref.at[d, c, r],
            dst_ref=got_ref.at[k - 1, d, c, r],
            send_sem=direct_send.at[k - 1, n],
            recv_sem=direct_recv.at[k - 1, n],
            device_id=at(-k),
            device_id_type=MESH,
        )

    def near(n, src, steps):
        d, c, r = pieces[n]
        return pltpu.make_async_remote_copy(
            src_ref=src.at[d, c, r],
            dst_ref=got_ref.at[0, d, c, r],
            send_sem=near_send.at[n],
            recv_sem=near_recv.at[n],
            device_id=at(steps),
            device_id_type=MESH,
        )

    def edge(k):
        return pltpu.make_async_remote_copy(
            src_ref=pack,
            dst_ref=edge_ref.at[k],
            send_sem=edge_send.at[k],
            recv_sem=edge_recv.at[k],
            device_id=at(-k, other=True),
            device_id_type=MESH,
        )

    total = range(len(pieces))
    edges = [edge(k) for k in range(reach + 1)]
    if relayed:
        for n in total:
            far(2, n).start()
            if n == 0:
                for e in edges:
                    e.start()

        @pl.when(even)
        def _():
            for n in total:
                far(2, n).wait_recv()
                near(n, got_ref.at[1], 1).start()
            for n in total:
                near(n, got_ref.at[1], 1).wait()

        @pl.when(jnp.logical_not(even))
        def _():
            for n in total:
                near(n, slc_ref, -1).start()
            for n in total:
                far(2, n).wait_recv()
            for n in total:
                near(n, slc_ref, -1).wait()

        for n in total:
            far(2, n).wait_send()
    else:
        for e in edges:
            e.start()
        for n in total:
            for k in range(1, reach + 1):
                far(k, n).start()
        for n in total:
            for k in range(1, reach + 1):
                far(k, n).wait()
    for e in edges:
        e.wait()


def exchange(slc, loop_size, reach):
    dates, parts, rows, columns = slc.shape
    pieces = dates * parts * (rows // PIECE)
    packed = -(-2 * dates * parts // 16) * 16
    return pl.pallas_call(
        functools.partial(exchange_kernel, loop_size, reach),
        out_shape=(
            jax.ShapeDtypeStruct((reach,) + slc.shape, jnp.bfloat16),
            jax.ShapeDtypeStruct((reach + 1, packed, columns), jnp.bfloat16),
        ),
        in_specs=[pl.BlockSpec(memory_space=pltpu.VMEM)],
        out_specs=(pl.BlockSpec(memory_space=pl.ANY), pl.BlockSpec(memory_space=pl.ANY)),
        scratch_shapes=[
            pltpu.VMEM((packed, columns), jnp.bfloat16),
            pltpu.SemaphoreType.DMA((reach, pieces)),
            pltpu.SemaphoreType.DMA((reach, pieces)),
            pltpu.SemaphoreType.DMA((pieces,)),
            pltpu.SemaphoreType.DMA((pieces,)),
            pltpu.SemaphoreType.DMA((reach + 1,)),
            pltpu.SemaphoreType.DMA((reach + 1,)),
        ],
        compiler_params=pltpu.CompilerParams(
            collective_id=0, has_side_effects=True, vmem_limit_bytes=16 << 20
        ),
        name="exchange",
    )(slc)


def shifted(tiles, by, lane):
    rolled = [pltpu.roll(t, by, 1) for t in tiles]
    shifted_tiles = [jnp.where(lane < by, 0.0, rolled[0])]
    for j in range(1, len(tiles)):
        shifted_tiles.append(jnp.where(lane < by, rolled[j - 1], rolled[j]))
    shifted_tiles.append(jnp.where(lane < by, rolled[-1], 0.0))
    return shifted_tiles


def box_columns(tiles, half, lane):
    count = len(tiles)
    zero = jnp.zeros_like(tiles[0])

    def add(x, y):
        x = x + [zero] * (count + 1 - len(x))
        return [a + b for a, b in zip(x, y[: count + 1])]

    two = add(tiles, shifted(tiles, 1, lane))
    three = add(two, shifted(tiles, 2, lane))
    four = add(two, shifted(two, 2, lane))
    seven = add(three, shifted(four, 3, lane))
    rest = [jnp.where(half == 3, 0.0, jnp.where(half == 4, a, b)) for a, b in zip(two, four)]
    return add(seven, shifted(rest, 7, lane))


def coherence_kernel(
    reach, total_dates, meta_ref, partner_ref, count_ref, width_ref, slc_ref, got_ref, edge_ref,
    out_ref, held, edges, ends, products, result, in_sem, out_sem,
):
    dates, parts, rows, columns = slc_ref.shape
    per_date = out_ref.shape[1]
    col_tiles = columns // LANES
    slots = dates * per_date
    first_date = meta_ref[0]
    row = meta_ref[1]
    copies = [
        pltpu.make_async_copy(slc_ref, held.at[pl.ds(0, dates)], in_sem.at[0]),
        pltpu.make_async_copy(edge_ref, edges, in_sem.at[1]),
    ]
    for k in range(reach):
        copies.append(
            pltpu.make_async_copy(got_ref.at[k], held.at[pl.ds((k + 1) * dates, dates)], in_sem.at[2 + k])
        )
    for copy in copies:
        copy.start()
    for copy in copies:
        copy.wait()

    for k in range(reach + 1):
        block = edges[k].astype(jnp.float32)
        for d in range(dates):
            for c in range(parts):
                at = (d * parts + c) * 2
                ends[k * dates + d, c, 0:2, :] = block[at : at + 2]
                ends[k * dates + d, c, 6:8, :] = block[at : at + 2]

    lane = lax.broadcasted_iota(jnp.int32, (16, LANES), 1)

    def write_products(at, count, u_re, u_im, v_re, v_im, keep=None):
        values = (
            u_re * v_re + u_im * v_im,
            u_im * v_re - u_re * v_im,
            u_re * u_re + u_im * u_im,
            v_re * v_re + v_im * v_im,
        )
        for q, value in enumerate(values):
            for j in range(col_tiles):
                part = value[:, j * LANES : (j + 1) * LANES]
                if keep is None:
                    products[q, j, at : at + count, :] = part
                else:
                    products[q, j, 0:8, :] = jnp.where(keep, part, 0.0)
                    products[q, j, rows + 8 : rows + 16, :] = jnp.where(keep, 0.0, part)

    def out_copy(slot):
        d, s = lax.div(slot, per_date), lax.rem(slot, per_date)
        return pltpu.make_async_copy(result.at[slot], out_ref.at[d, s], out_sem.at[slot])

    def one_slot(slot, carry):
        d, s = lax.div(slot, per_date), lax.rem(slot, per_date)
        used = s < count_ref[d]

        @pl.when(used)
        def _():
            v = lax.rem(partner_ref[d, s] - first_date + total_dates, total_dates)
            half = width_ref[d, s]
            write_products(0, 8, ends[d, 0], ends[d, 1], ends[v, 0], ends[v, 1], row == 1)
            for r in range(0, rows, 16):
                write_products(
                    8 + r, 16,
                    *(
                        held[x, c, r : r + 16, :].astype(jnp.float32)
                        for x in (d, v)
                        for c in range(2)
                    ),
                )
            for r in range(0, rows, 16):
                sums = []
                for q in range(4):
                    tiles = []
                    for j in range(col_tiles):
                        taken = [products[q, j, r + 6 + k : r + 22 + k, :] for k in range(5)]
                        tiles.append((taken[0] + taken[1]) + (taken[2] + taken[3]) + taken[4])
                    sums.append(box_columns(tiles, half, lane))
                ratio = [
                    jnp.sqrt(a * a + b * b) * lax.rsqrt(u * w) for a, b, u, w in zip(*sums)
                ]
                back = [pltpu.roll(x, LANES - half, 1) for x in ratio]
                for j in range(col_tiles):
                    value = jnp.where(lane < LANES - half, back[j], back[j + 1])
                    result[slot, r : r + 16, j * LANES : (j + 1) * LANES] = value.astype(jnp.bfloat16)

        @pl.when(jnp.logical_not(used))
        def _():
            result[slot] = jnp.zeros((rows, columns), jnp.bfloat16)

        out_copy(slot).start()
        return carry

    lax.fori_loop(0, slots, one_slot, 0)
    for slot in range(slots):
        out_copy(slot).wait()


def coherence(meta, partners, counts, windows, slc, got, edge, reach, total_dates):
    dates, parts, rows, columns = slc.shape
    per_date = partners.shape[1]
    held = dates * (reach + 1)
    smem = pl.BlockSpec(memory_space=pltpu.SMEM)
    anywhere = pl.BlockSpec(memory_space=pl.ANY)
    return pl.pallas_call(
        functools.partial(coherence_kernel, reach, total_dates),
        out_shape=jax.ShapeDtypeStruct((dates, per_date, rows, columns), jnp.bfloat16),
        in_specs=[smem] * 4 + [anywhere] * 3,
        out_specs=anywhere,
        scratch_shapes=[
            pltpu.VMEM((held, parts, rows, columns), jnp.bfloat16),
            pltpu.VMEM(edge.shape, jnp.bfloat16),
            pltpu.VMEM((held, parts, 8, columns), jnp.float32),
            pltpu.VMEM((4, columns // LANES, rows + 16, LANES), jnp.float32),
            pltpu.VMEM((dates * per_date, rows, columns), jnp.bfloat16),
            pltpu.SemaphoreType.DMA((reach + 2,)),
            pltpu.SemaphoreType.DMA((dates * per_date,)),
        ],
        compiler_params=pltpu.CompilerParams(vmem_limit_bytes=40 << 20),
        name="coherence",
    )(meta, partners, counts, windows, slc, got, edge)


def local(slc_stack, partners, counts, windows):
    dates = slc_stack.shape[0]
    loop_size = lax.axis_size("date")
    reach = loop_size // 4
    total_dates = dates * loop_size
    meta = jnp.stack([lax.axis_index("date") * dates, lax.axis_index("row")]).astype(jnp.int32)
    got, edge = exchange(slc_stack, loop_size, reach)
    return coherence(meta, partners, counts, windows, slc_stack, got, edge, reach, total_dates)


def solution(mesh):
    in_specs = (
        P("date", None, ("tiles", "row"), None),
        P("date", None),
        P("date"),
        P("date", None),
    )
    out_specs = P("date", None, ("tiles", "row"), None)
    return jax.shard_map(local, mesh=mesh, in_specs=in_specs, out_specs=out_specs, check_vma=False)
```

```python
import functools
import jax
import jax.numpy as jnp
from jax import lax
from jax.experimental import pallas as pl
from jax.experimental.pallas import tpu as pltpu
from jax.sharding import PartitionSpec as P

MESH = pl.DeviceIdType.MESH
LANES = 128
PIECE = 32
BLOCK = 256
HALVES = (3, 4, 5)


def exchange_kernel(loop_size, reach, slc_ref, got_ref, edge_ref, pack, *sems):
    direct_send, direct_recv, near_send, near_recv, edge_send, edge_recv = sems
    dates, parts, rows, columns = slc_ref.shape
    tile = lax.axis_index("tiles")
    me = lax.axis_index("date")
    row = lax.axis_index("row")
    pieces = [
        (d, c, pl.ds(r, PIECE)) for d in range(dates) for c in range(parts) for r in range(0, rows, PIECE)
    ]
    relayed = reach == 2

    def at(steps, other=False):
        there = lax.rem(me + steps + loop_size, loop_size)
        return (tile, there, 1 - row if other else row)

    barrier = pltpu.get_barrier_semaphore()

    def greet(device):
        pl.semaphore_signal(barrier, inc=1, device_id=device, device_id_type=MESH)

    even = lax.rem(me, 2) == 0
    for k in range(reach + 1):
        greet(at(k, other=True))
    if relayed:
        greet(at(2))
        greet(at(jnp.where(even, 1, -1)))
    else:
        for k in range(1, reach + 1):
            greet(at(k))

    picked = []
    for d in range(dates):
        for c in range(parts):
            last = slc_ref[d, c, rows - 16 : rows, :].astype(jnp.float32)[14:16]
            first = slc_ref[d, c, 0:16, :].astype(jnp.float32)[0:2]
            picked.append(jnp.where(row == 0, last, first))
    spare = pack.shape[0] - 2 * len(picked)
    if spare:
        picked.append(jnp.zeros((spare, columns), jnp.float32))
    pack[...] = jnp.concatenate(picked, axis=0).astype(jnp.bfloat16)

    pl.semaphore_wait(barrier, 2 * reach + 1)

    def far(k, n):
        d, c, r = pieces[n]
        return pltpu.make_async_remote_copy(
            src_ref=slc_ref.at[d, c, r],
            dst_ref=got_ref.at[k - 1, d, c, r],
            send_sem=direct_send.at[k - 1, n],
            recv_sem=direct_recv.at[k - 1, n],
            device_id=at(-k),
            device_id_type=MESH,
        )

    def near(n, src, steps):
        d, c, r = pieces[n]
        return pltpu.make_async_remote_copy(
            src_ref=src.at[d, c, r],
            dst_ref=got_ref.at[0, d, c, r],
            send_sem=near_send.at[n],
            recv_sem=near_recv.at[n],
            device_id=at(steps),
            device_id_type=MESH,
        )

    def edge(k):
        return pltpu.make_async_remote_copy(
            src_ref=pack,
            dst_ref=edge_ref.at[k],
            send_sem=edge_send.at[k],
            recv_sem=edge_recv.at[k],
            device_id=at(-k, other=True),
            device_id_type=MESH,
        )

    total = range(len(pieces))
    edges = [edge(k) for k in range(reach + 1)]
    if relayed:
        for n in total:
            far(2, n).start()
            if n == 0:
                for e in edges:
                    e.start()

        @pl.when(even)
        def _():
            for n in total:
                far(2, n).wait_recv()
                near(n, got_ref.at[1], 1).start()
            for n in total:
                near(n, got_ref.at[1], 1).wait()

        @pl.when(jnp.logical_not(even))
        def _():
            for n in total:
                near(n, slc_ref, -1).start()
            for n in total:
                far(2, n).wait_recv()
            for n in total:
                near(n, slc_ref, -1).wait()

        for n in total:
            far(2, n).wait_send()
    else:
        for e in edges:
            e.start()
        for n in total:
            for k in range(1, reach + 1):
                far(k, n).start()
        for n in total:
            for k in range(1, reach + 1):
                far(k, n).wait()
    for e in edges:
        e.wait()


def exchange(slc, loop_size, reach):
    dates, parts, rows, columns = slc.shape
    pieces = dates * parts * (rows // PIECE)
    packed = -(-2 * dates * parts // 16) * 16
    return pl.pallas_call(
        functools.partial(exchange_kernel, loop_size, reach),
        out_shape=(
            jax.ShapeDtypeStruct((reach,) + slc.shape, jnp.bfloat16),
            jax.ShapeDtypeStruct((reach + 1, packed, columns), jnp.bfloat16),
        ),
        in_specs=[pl.BlockSpec(memory_space=pltpu.VMEM)],
        out_specs=(pl.BlockSpec(memory_space=pl.ANY), pl.BlockSpec(memory_space=pl.ANY)),
        scratch_shapes=[
            pltpu.VMEM((packed, columns), jnp.bfloat16),
            pltpu.SemaphoreType.DMA((reach, pieces)),
            pltpu.SemaphoreType.DMA((reach, pieces)),
            pltpu.SemaphoreType.DMA((pieces,)),
            pltpu.SemaphoreType.DMA((pieces,)),
            pltpu.SemaphoreType.DMA((reach + 1,)),
            pltpu.SemaphoreType.DMA((reach + 1,)),
        ],
        compiler_params=pltpu.CompilerParams(
            collective_id=0, has_side_effects=True, vmem_limit_bytes=16 << 20
        ),
        name="exchange",
    )(slc)


def band(half, block):
    into = lax.broadcasted_iota(jnp.int32, (2 * block, block), 0) - block // 2
    out = lax.broadcasted_iota(jnp.int32, (2 * block, block), 1)
    return jnp.where(jnp.abs(into - out) <= half, 1.0, 0.0).astype(jnp.bfloat16)


def coherence_kernel(
    reach, total_dates, meta_ref, partner_ref, count_ref, width_ref, slc_ref, got_ref, edge_ref,
    out_ref, held, edges, ends, products, bands, split, result, in_sem, out_sem,
):
    dates, parts, rows, columns = slc_ref.shape
    per_date = out_ref.shape[1]
    col_tiles = columns // LANES
    slots = dates * per_date
    first_date = meta_ref[0]
    row = meta_ref[1]
    copies = [
        pltpu.make_async_copy(slc_ref, held.at[pl.ds(0, dates)], in_sem.at[0]),
        pltpu.make_async_copy(edge_ref, edges, in_sem.at[1]),
    ]
    for k in range(reach):
        copies.append(
            pltpu.make_async_copy(got_ref.at[k], held.at[pl.ds((k + 1) * dates, dates)], in_sem.at[2 + k])
        )
    for copy in copies:
        copy.start()
    for half in HALVES:
        matrix = band(half, BLOCK)
        bands[half - HALVES[0], 0 : 2 * BLOCK, :] = matrix
        bands[half - HALVES[0], 2 * BLOCK : 4 * BLOCK, :] = matrix
    side = BLOCK // 2
    zeros = jnp.zeros((2, 4 * rows, side), jnp.bfloat16)
    split[:, :, 0:side] = zeros
    split[:, :, side + columns : 2 * side + columns] = zeros
    for copy in copies:
        copy.wait()

    for k in range(reach + 1):
        block = edges[k].astype(jnp.float32)
        for d in range(dates):
            for c in range(parts):
                at = (d * parts + c) * 2
                ends[k * dates + d, c, 0:2, :] = block[at : at + 2]
                ends[k * dates + d, c, 6:8, :] = block[at : at + 2]

    def write_products(at, count, u_re, u_im, v_re, v_im, keep=None):
        values = (
            u_re * v_re + u_im * v_im,
            u_im * v_re - u_re * v_im,
            u_re * u_re + u_im * u_im,
            v_re * v_re + v_im * v_im,
        )
        for q, value in enumerate(values):
            for j in range(col_tiles):
                part = value[:, j * LANES : (j + 1) * LANES]
                if keep is None:
                    products[q, j, at : at + count, :] = part
                else:
                    products[q, j, 0:8, :] = jnp.where(keep, part, 0.0)
                    products[q, j, rows + 8 : rows + 16, :] = jnp.where(keep, 0.0, part)

    def out_copy(slot):
        d, s = lax.div(slot, per_date), lax.rem(slot, per_date)
        return pltpu.make_async_copy(result.at[slot], out_ref.at[d, s], out_sem.at[slot])

    def one_slot(slot, carry):
        d, s = lax.div(slot, per_date), lax.rem(slot, per_date)
        used = s < count_ref[d]

        @pl.when(used)
        def _():
            v = lax.rem(partner_ref[d, s] - first_date + total_dates, total_dates)
            half = width_ref[d, s]
            write_products(0, 8, ends[d, 0], ends[d, 1], ends[v, 0], ends[v, 1], row == 1)
            for r in range(0, rows, 16):
                write_products(
                    8 + r, 16,
                    *(
                        held[x, c, r : r + 16, :].astype(jnp.float32)
                        for x in (d, v)
                        for c in range(2)
                    ),
                )
            for q in range(4):
                for r in range(0, rows, 16):
                    for j in range(col_tiles):
                        taken = [products[q, j, r + 6 + k : r + 22 + k, :] for k in range(5)]
                        total = (taken[0] + taken[1]) + (taken[2] + taken[3]) + taken[4]
                        high = total.astype(jnp.bfloat16)
                        low = (total - high.astype(jnp.float32)).astype(jnp.bfloat16)
                        at = side + j * LANES
                        split[0, q * rows + r : q * rows + r + 16, at : at + LANES] = high
                        split[1, q * rows + r : q * rows + r + 16, at : at + LANES] = low
            matrix = bands[half - HALVES[0]]
            for c in range(0, columns, BLOCK):
                window = jnp.concatenate(
                    [split[0, :, c : c + 2 * BLOCK], split[1, :, c : c + 2 * BLOCK]], axis=1
                )
                box = jnp.dot(window, matrix, preferred_element_type=jnp.float32)
                box_re, box_im, box_u, box_v = (box[q * rows : (q + 1) * rows] for q in range(4))
                value = jnp.sqrt(box_re * box_re + box_im * box_im) * lax.rsqrt(box_u * box_v)
                result[slot, :, c : c + BLOCK] = value.astype(jnp.bfloat16)

        @pl.when(jnp.logical_not(used))
        def _():
            result[slot] = jnp.zeros((rows, columns), jnp.bfloat16)

        out_copy(slot).start()
        return carry

    lax.fori_loop(0, slots, one_slot, 0)
    for slot in range(slots):
        out_copy(slot).wait()


def coherence(meta, partners, counts, windows, slc, got, edge, reach, total_dates):
    dates, parts, rows, columns = slc.shape
    per_date = partners.shape[1]
    held = dates * (reach + 1)
    smem = pl.BlockSpec(memory_space=pltpu.SMEM)
    anywhere = pl.BlockSpec(memory_space=pl.ANY)
    return pl.pallas_call(
        functools.partial(coherence_kernel, reach, total_dates),
        out_shape=jax.ShapeDtypeStruct((dates, per_date, rows, columns), jnp.bfloat16),
        in_specs=[smem] * 4 + [anywhere] * 3,
        out_specs=anywhere,
        scratch_shapes=[
            pltpu.VMEM((held, parts, rows, columns), jnp.bfloat16),
            pltpu.VMEM(edge.shape, jnp.bfloat16),
            pltpu.VMEM((held, parts, 8, columns), jnp.float32),
            pltpu.VMEM((4, columns // LANES, rows + 16, LANES), jnp.float32),
            pltpu.VMEM((len(HALVES), 4 * BLOCK, BLOCK), jnp.bfloat16),
            pltpu.VMEM((2, 4 * rows, columns + BLOCK), jnp.bfloat16),
            pltpu.VMEM((dates * per_date, rows, columns), jnp.bfloat16),
            pltpu.SemaphoreType.DMA((reach + 2,)),
            pltpu.SemaphoreType.DMA((dates * per_date,)),
        ],
        compiler_params=pltpu.CompilerParams(vmem_limit_bytes=40 << 20),
        name="coherence",
    )(meta, partners, counts, windows, slc, got, edge)


def local(slc_stack, partners, counts, windows):
    dates = slc_stack.shape[0]
    loop_size = lax.axis_size("date")
    reach = loop_size // 4
    total_dates = dates * loop_size
    meta = jnp.stack([lax.axis_index("date") * dates, lax.axis_index("row")]).astype(jnp.int32)
    got, edge = exchange(slc_stack, loop_size, reach)
    return coherence(meta, partners, counts, windows, slc_stack, got, edge, reach, total_dates)


def solution(mesh):
    in_specs = (
        P("date", None, ("tiles", "row"), None),
        P("date", None),
        P("date"),
        P("date", None),
    )
    out_specs = P("date", None, ("tiles", "row"), None)
    return jax.shard_map(local, mesh=mesh, in_specs=in_specs, out_specs=out_specs, check_vma=False)
```

```python
import functools
import jax
import jax.numpy as jnp
from jax import lax
from jax.experimental import pallas as pl
from jax.experimental.pallas import tpu as pltpu
from jax.sharding import PartitionSpec as P

MESH = pl.DeviceIdType.MESH
LANES = 128
PIECE = 32
BLOCK = 256
HALVES = (3, 4, 5)


def exchange_kernel(loop_size, reach, slc_ref, got_ref, edge_ref, rim, pack, *sems):
    rim_sem, direct_send, direct_recv, near_send, near_recv, edge_send, edge_recv = sems
    dates, parts, rows, columns = slc_ref.shape
    tile = lax.axis_index("tiles")
    me = lax.axis_index("date")
    row = lax.axis_index("row")
    pieces = [
        (d, c, pl.ds(r, PIECE)) for d in range(dates) for c in range(parts) for r in range(0, rows, PIECE)
    ]
    relayed = reach == 2

    def at(steps, other=False):
        there = lax.rem(me + steps + loop_size, loop_size)
        return (tile, there, 1 - row if other else row)

    barrier = pltpu.get_barrier_semaphore()

    def greet(device):
        pl.semaphore_signal(barrier, inc=1, device_id=device, device_id_type=MESH)

    even = lax.rem(me, 2) == 0
    for k in range(reach + 1):
        greet(at(k, other=True))
    if relayed:
        greet(at(2))
        greet(at(jnp.where(even, 1, -1)))
    else:
        for k in range(1, reach + 1):
            greet(at(k))

    start = pl.multiple_of((1 - row) * (rows - 16), 16)
    rim_copy = pltpu.make_async_copy(slc_ref.at[:, :, pl.ds(start, 16), :], rim, rim_sem)
    rim_copy.start()
    rim_copy.wait()
    picked = []
    for d in range(dates):
        for c in range(parts):
            near_rows = rim[d, c].astype(jnp.float32)
            picked.append(jnp.where(row == 0, near_rows[14:16], near_rows[0:2]))
    spare = pack.shape[0] - 2 * len(picked)
    if spare:
        picked.append(jnp.zeros((spare, columns), jnp.float32))
    pack[...] = jnp.concatenate(picked, axis=0).astype(jnp.bfloat16)

    pl.semaphore_wait(barrier, 2 * reach + 1)

    def far(k, n):
        d, c, r = pieces[n]
        return pltpu.make_async_remote_copy(
            src_ref=slc_ref.at[d, c, r],
            dst_ref=got_ref.at[k - 1, d, c, r],
            send_sem=direct_send.at[k - 1, n],
            recv_sem=direct_recv.at[k - 1, n],
            device_id=at(-k),
            device_id_type=MESH,
        )

    def near(n, src, steps):
        d, c, r = pieces[n]
        return pltpu.make_async_remote_copy(
            src_ref=src.at[d, c, r],
            dst_ref=got_ref.at[0, d, c, r],
            send_sem=near_send.at[n],
            recv_sem=near_recv.at[n],
            device_id=at(steps),
            device_id_type=MESH,
        )

    def edge(k):
        return pltpu.make_async_remote_copy(
            src_ref=pack,
            dst_ref=edge_ref.at[k],
            send_sem=edge_send.at[k],
            recv_sem=edge_recv.at[k],
            device_id=at(-k, other=True),
            device_id_type=MESH,
        )

    total = range(len(pieces))
    edges = [edge(k) for k in range(reach + 1)]
    if relayed:
        for n in total:
            far(2, n).start()
            if n == 0:
                for e in edges:
                    e.start()

        @pl.when(even)
        def _():
            for n in total:
                far(2, n).wait_recv()
                near(n, got_ref.at[1], 1).start()
            for n in total:
                near(n, got_ref.at[1], 1).wait()

        @pl.when(jnp.logical_not(even))
        def _():
            for n in total:
                near(n, slc_ref, -1).start()
            for n in total:
                far(2, n).wait_recv()
            for n in total:
                near(n, slc_ref, -1).wait()

        for n in total:
            far(2, n).wait_send()
    else:
        for e in edges:
            e.start()
        for n in total:
            for k in range(1, reach + 1):
                far(k, n).start()
        for n in total:
            for k in range(1, reach + 1):
                far(k, n).wait()
    for e in edges:
        e.wait()


def exchange(slc, loop_size, reach):
    dates, parts, rows, columns = slc.shape
    pieces = dates * parts * (rows // PIECE)
    packed = -(-2 * dates * parts // 16) * 16
    return pl.pallas_call(
        functools.partial(exchange_kernel, loop_size, reach),
        out_shape=(
            jax.ShapeDtypeStruct((reach,) + slc.shape, jnp.bfloat16),
            jax.ShapeDtypeStruct((reach + 1, packed, columns), jnp.bfloat16),
        ),
        in_specs=[pl.BlockSpec(memory_space=pl.ANY)],
        out_specs=(pl.BlockSpec(memory_space=pl.ANY), pl.BlockSpec(memory_space=pl.ANY)),
        scratch_shapes=[
            pltpu.VMEM((dates, parts, 16, columns), jnp.bfloat16),
            pltpu.VMEM((packed, columns), jnp.bfloat16),
            pltpu.SemaphoreType.DMA,
            pltpu.SemaphoreType.DMA((reach, pieces)),
            pltpu.SemaphoreType.DMA((reach, pieces)),
            pltpu.SemaphoreType.DMA((pieces,)),
            pltpu.SemaphoreType.DMA((pieces,)),
            pltpu.SemaphoreType.DMA((reach + 1,)),
            pltpu.SemaphoreType.DMA((reach + 1,)),
        ],
        compiler_params=pltpu.CompilerParams(
            collective_id=0, has_side_effects=True, vmem_limit_bytes=16 << 20
        ),
        name="exchange",
    )(slc)


def band(half, block):
    into = lax.broadcasted_iota(jnp.int32, (2 * block, block), 0) - block // 2
    out = lax.broadcasted_iota(jnp.int32, (2 * block, block), 1)
    return jnp.where(jnp.abs(into - out) <= half, 1.0, 0.0).astype(jnp.bfloat16)


def coherence_kernel(
    reach, total_dates, partner_hbm, count_hbm, width_hbm, slc_ref, got_ref, edge_ref,
    out_ref, held, edges, ends, products, bands, split, result,
    partner_ref, count_ref, width_ref, in_sem, out_sem,
):
    dates, parts, rows, columns = slc_ref.shape
    per_date = out_ref.shape[1]
    col_tiles = columns // LANES
    slots = dates * per_date
    first_date = lax.axis_index("date") * dates
    row = lax.axis_index("row")
    copies = [
        pltpu.make_async_copy(slc_ref, held.at[pl.ds(0, dates)], in_sem.at[0]),
        pltpu.make_async_copy(edge_ref, edges, in_sem.at[1]),
    ]
    for k in range(reach):
        copies.append(
            pltpu.make_async_copy(got_ref.at[k], held.at[pl.ds((k + 1) * dates, dates)], in_sem.at[2 + k])
        )
    scalars = ((partner_hbm, partner_ref), (count_hbm, count_ref), (width_hbm, width_ref))
    for n, (src, dst) in enumerate(scalars):
        copies.append(pltpu.make_async_copy(src, dst, in_sem.at[2 + reach + n]))
    for copy in copies:
        copy.start()
    for half in HALVES:
        matrix = band(half, BLOCK)
        bands[half - HALVES[0], 0 : 2 * BLOCK, :] = matrix
        bands[half - HALVES[0], 2 * BLOCK : 4 * BLOCK, :] = matrix
    side = BLOCK // 2
    zeros = jnp.zeros((2, 4 * rows, side), jnp.bfloat16)
    split[:, :, 0:side] = zeros
    split[:, :, side + columns : 2 * side + columns] = zeros
    for copy in copies:
        copy.wait()

    for k in range(reach + 1):
        block = edges[k].astype(jnp.float32)
        for d in range(dates):
            for c in range(parts):
                at = (d * parts + c) * 2
                ends[k * dates + d, c, 0:2, :] = block[at : at + 2]
                ends[k * dates + d, c, 6:8, :] = block[at : at + 2]

    def write_products(at, count, u_re, u_im, v_re, v_im, keep=None):
        values = (
            u_re * v_re + u_im * v_im,
            u_im * v_re - u_re * v_im,
            u_re * u_re + u_im * u_im,
            v_re * v_re + v_im * v_im,
        )
        for q, value in enumerate(values):
            for j in range(col_tiles):
                part = value[:, j * LANES : (j + 1) * LANES]
                if keep is None:
                    products[q, j, at : at + count, :] = part
                else:
                    products[q, j, 0:8, :] = jnp.where(keep, part, 0.0)
                    products[q, j, rows + 8 : rows + 16, :] = jnp.where(keep, 0.0, part)

    def out_copy(slot):
        d, s = lax.div(slot, per_date), lax.rem(slot, per_date)
        return pltpu.make_async_copy(result.at[slot], out_ref.at[d, s], out_sem.at[slot])

    def one_slot(slot, carry):
        d, s = lax.div(slot, per_date), lax.rem(slot, per_date)
        used = s < count_ref[d]

        @pl.when(used)
        def _():
            v = lax.rem(partner_ref[d, s] - first_date + total_dates, total_dates)
            half = width_ref[d, s]
            write_products(0, 8, ends[d, 0], ends[d, 1], ends[v, 0], ends[v, 1], row == 1)
            for r in range(0, rows, 16):
                write_products(
                    8 + r, 16,
                    *(
                        held[x, c, r : r + 16, :].astype(jnp.float32)
                        for x in (d, v)
                        for c in range(2)
                    ),
                )
            for q in range(4):
                for r in range(0, rows, 16):
                    for j in range(col_tiles):
                        taken = [products[q, j, r + 6 + k : r + 22 + k, :] for k in range(5)]
                        total = (taken[0] + taken[1]) + (taken[2] + taken[3]) + taken[4]
                        high = total.astype(jnp.bfloat16)
                        low = (total - high.astype(jnp.float32)).astype(jnp.bfloat16)
                        at = side + j * LANES
                        split[0, q * rows + r : q * rows + r + 16, at : at + LANES] = high
                        split[1, q * rows + r : q * rows + r + 16, at : at + LANES] = low
            matrix = bands[half - HALVES[0]]
            for c in range(0, columns, BLOCK):
                window = jnp.concatenate(
                    [split[0, :, c : c + 2 * BLOCK], split[1, :, c : c + 2 * BLOCK]], axis=1
                )
                box = jnp.dot(window, matrix, preferred_element_type=jnp.float32)
                box_re, box_im, box_u, box_v = (box[q * rows : (q + 1) * rows] for q in range(4))
                value = jnp.sqrt(box_re * box_re + box_im * box_im) * lax.rsqrt(box_u * box_v)
                result[slot, :, c : c + BLOCK] = value.astype(jnp.bfloat16)

        @pl.when(jnp.logical_not(used))
        def _():
            result[slot] = jnp.zeros((rows, columns), jnp.bfloat16)

        out_copy(slot).start()
        return carry

    lax.fori_loop(0, slots, one_slot, 0)
    for slot in range(slots):
        out_copy(slot).wait()


def coherence(partners, counts, windows, slc, got, edge, reach, total_dates):
    dates, parts, rows, columns = slc.shape
    per_date = partners.shape[1]
    held = dates * (reach + 1)
    anywhere = pl.BlockSpec(memory_space=pl.ANY)
    return pl.pallas_call(
        functools.partial(coherence_kernel, reach, total_dates),
        out_shape=jax.ShapeDtypeStruct((dates, per_date, rows, columns), jnp.bfloat16),
        in_specs=[anywhere] * 6,
        out_specs=anywhere,
        scratch_shapes=[
            pltpu.VMEM((held, parts, rows, columns), jnp.bfloat16),
            pltpu.VMEM(edge.shape, jnp.bfloat16),
            pltpu.VMEM((held, parts, 8, columns), jnp.float32),
            pltpu.VMEM((4, columns // LANES, rows + 16, LANES), jnp.float32),
            pltpu.VMEM((len(HALVES), 4 * BLOCK, BLOCK), jnp.bfloat16),
            pltpu.VMEM((2, 4 * rows, columns + BLOCK), jnp.bfloat16),
            pltpu.VMEM((dates * per_date, rows, columns), jnp.bfloat16),
            pltpu.SMEM(partners.shape, jnp.int32),
            pltpu.SMEM(counts.shape, jnp.int32),
            pltpu.SMEM(windows.shape, jnp.int32),
            pltpu.SemaphoreType.DMA((reach + 5,)),
            pltpu.SemaphoreType.DMA((dates * per_date,)),
        ],
        compiler_params=pltpu.CompilerParams(vmem_limit_bytes=40 << 20),
        name="coherence",
    )(partners, counts, windows, slc, got, edge)


def local(slc_stack, partners, counts, windows):
    dates = slc_stack.shape[0]
    loop_size = lax.axis_size("date")
    reach = loop_size // 4
    total_dates = dates * loop_size
    got, edge = exchange(slc_stack, loop_size, reach)
    return coherence(partners, counts, windows, slc_stack, got, edge, reach, total_dates)


def solution(mesh):
    in_specs = (
        P("date", None, ("tiles", "row"), None),
        P("date", None),
        P("date"),
        P("date", None),
    )
    out_specs = P("date", None, ("tiles", "row"), None)
    return jax.shard_map(local, mesh=mesh, in_specs=in_specs, out_specs=out_specs, check_vma=False)
```

```python
import functools
import jax
import jax.numpy as jnp
from jax import lax
from jax.experimental import pallas as pl
from jax.experimental.pallas import tpu as pltpu
from jax.sharding import PartitionSpec as P

MESH = pl.DeviceIdType.MESH
LANES = 128
PIECE = 32
BLOCK = 256
HALVES = (3, 4, 5)


def exchange_kernel(loop_size, reach, slc_ref, got_ref, edge_ref, rim, pack, *sems):
    rim_sem, own_sem, direct_send, direct_recv, near_send, near_recv, edge_send, edge_recv = sems
    dates, parts, rows, columns = slc_ref.shape
    tile = lax.axis_index("tiles")
    me = lax.axis_index("date")
    row = lax.axis_index("row")
    pieces = [
        (d, c, pl.ds(r, PIECE)) for d in range(dates) for c in range(parts) for r in range(0, rows, PIECE)
    ]
    relayed = reach == 2

    def at(steps, other=False):
        there = lax.rem(me + steps + loop_size, loop_size)
        return (tile, there, 1 - row if other else row)

    barrier = pltpu.get_barrier_semaphore()

    def greet(device):
        pl.semaphore_signal(barrier, inc=1, device_id=device, device_id_type=MESH)

    even = lax.rem(me, 2) == 0
    for k in range(reach + 1):
        greet(at(k, other=True))
    if relayed:
        greet(at(2))
        greet(at(jnp.where(even, 1, -1)))
    else:
        for k in range(1, reach + 1):
            greet(at(k))

    start = pl.multiple_of((1 - row) * (rows - 16), 16)
    rim_copy = pltpu.make_async_copy(slc_ref.at[:, :, pl.ds(start, 16), :], rim, rim_sem)
    rim_copy.start()
    rim_copy.wait()
    picked = []
    for d in range(dates):
        for c in range(parts):
            near_rows = rim[d, c].astype(jnp.float32)
            picked.append(jnp.where(row == 0, near_rows[14:16], near_rows[0:2]))
    spare = pack.shape[0] - 2 * len(picked)
    if spare:
        picked.append(jnp.zeros((spare, columns), jnp.float32))
    pack[...] = jnp.concatenate(picked, axis=0).astype(jnp.bfloat16)

    pl.semaphore_wait(barrier, 2 * reach + 1)

    def far(k, n):
        d, c, r = pieces[n]
        return pltpu.make_async_remote_copy(
            src_ref=slc_ref.at[d, c, r],
            dst_ref=got_ref.at[k, d, c, r],
            send_sem=direct_send.at[k - 1, n],
            recv_sem=direct_recv.at[k - 1, n],
            device_id=at(-k),
            device_id_type=MESH,
        )

    def near(n, src, steps):
        d, c, r = pieces[n]
        return pltpu.make_async_remote_copy(
            src_ref=src.at[d, c, r],
            dst_ref=got_ref.at[1, d, c, r],
            send_sem=near_send.at[n],
            recv_sem=near_recv.at[n],
            device_id=at(steps),
            device_id_type=MESH,
        )

    def edge(k):
        return pltpu.make_async_remote_copy(
            src_ref=pack,
            dst_ref=edge_ref.at[k],
            send_sem=edge_send.at[k],
            recv_sem=edge_recv.at[k],
            device_id=at(-k, other=True),
            device_id_type=MESH,
        )

    total = range(len(pieces))
    edges = [edge(k) for k in range(reach + 1)]
    own_copy = pltpu.make_async_copy(slc_ref, got_ref.at[0], own_sem)
    if relayed:
        for n in total:
            far(2, n).start()
            if n == 0:
                for e in edges:
                    e.start()

        own_copy.start()

        @pl.when(even)
        def _():
            for n in total:
                far(2, n).wait_recv()
                near(n, got_ref.at[2], 1).start()
            for n in total:
                near(n, got_ref.at[2], 1).wait()

        @pl.when(jnp.logical_not(even))
        def _():
            for n in total:
                near(n, slc_ref, -1).start()
            for n in total:
                far(2, n).wait_recv()
            for n in total:
                near(n, slc_ref, -1).wait()

        for n in total:
            far(2, n).wait_send()
    else:
        own_copy.start()
        for e in edges:
            e.start()
        for n in total:
            for k in range(1, reach + 1):
                far(k, n).start()
        for n in total:
            for k in range(1, reach + 1):
                far(k, n).wait()
    for e in edges:
        e.wait()
    own_copy.wait()


def exchange(slc, loop_size, reach):
    dates, parts, rows, columns = slc.shape
    pieces = dates * parts * (rows // PIECE)
    packed = -(-2 * dates * parts // 16) * 16
    return pl.pallas_call(
        functools.partial(exchange_kernel, loop_size, reach),
        out_shape=(
            jax.ShapeDtypeStruct((reach + 1,) + slc.shape, jnp.bfloat16),
            jax.ShapeDtypeStruct((reach + 1, packed, columns), jnp.bfloat16),
        ),
        in_specs=[pl.BlockSpec(memory_space=pltpu.HBM)],
        out_specs=(pl.BlockSpec(memory_space=pl.ANY), pl.BlockSpec(memory_space=pl.ANY)),
        scratch_shapes=[
            pltpu.VMEM((dates, parts, 16, columns), jnp.bfloat16),
            pltpu.VMEM((packed, columns), jnp.bfloat16),
            pltpu.SemaphoreType.DMA,
            pltpu.SemaphoreType.DMA,
            pltpu.SemaphoreType.DMA((reach, pieces)),
            pltpu.SemaphoreType.DMA((reach, pieces)),
            pltpu.SemaphoreType.DMA((pieces,)),
            pltpu.SemaphoreType.DMA((pieces,)),
            pltpu.SemaphoreType.DMA((reach + 1,)),
            pltpu.SemaphoreType.DMA((reach + 1,)),
        ],
        compiler_params=pltpu.CompilerParams(
            collective_id=0, has_side_effects=True, vmem_limit_bytes=16 << 20
        ),
        name="exchange",
    )(slc)


def band(half, block):
    into = lax.broadcasted_iota(jnp.int32, (2 * block, block), 0) - block // 2
    out = lax.broadcasted_iota(jnp.int32, (2 * block, block), 1)
    return jnp.where(jnp.abs(into - out) <= half, 1.0, 0.0).astype(jnp.bfloat16)


def coherence_kernel(
    reach, total_dates, partner_hbm, count_hbm, width_hbm, held, edges,
    out_ref, ends, products, bands, split, result,
    partner_ref, count_ref, width_ref, in_sem, out_sem,
):
    blocks, dates, parts, rows, columns = held.shape
    per_date = out_ref.shape[1]
    col_tiles = columns // LANES
    slots = dates * per_date
    first_date = lax.axis_index("date") * dates
    row = lax.axis_index("row")
    copies = []
    scalars = ((partner_hbm, partner_ref), (count_hbm, count_ref), (width_hbm, width_ref))
    for n, (src, dst) in enumerate(scalars):
        copies.append(pltpu.make_async_copy(src, dst, in_sem.at[n]))
    for copy in copies:
        copy.start()
    for half in HALVES:
        matrix = band(half, BLOCK)
        bands[half - HALVES[0], 0 : 2 * BLOCK, :] = matrix
        bands[half - HALVES[0], 2 * BLOCK : 4 * BLOCK, :] = matrix
    side = BLOCK // 2
    zeros = jnp.zeros((2, 4 * rows, side), jnp.bfloat16)
    split[:, :, 0:side] = zeros
    split[:, :, side + columns : 2 * side + columns] = zeros
    for copy in copies:
        copy.wait()

    for k in range(reach + 1):
        block = edges[k].astype(jnp.float32)
        for d in range(dates):
            for c in range(parts):
                at = (d * parts + c) * 2
                ends[k * dates + d, c, 0:2, :] = block[at : at + 2]
                ends[k * dates + d, c, 6:8, :] = block[at : at + 2]

    def write_products(at, count, u_re, u_im, v_re, v_im, keep=None):
        values = (
            u_re * v_re + u_im * v_im,
            u_im * v_re - u_re * v_im,
            u_re * u_re + u_im * u_im,
            v_re * v_re + v_im * v_im,
        )
        for q, value in enumerate(values):
            for j in range(col_tiles):
                part = value[:, j * LANES : (j + 1) * LANES]
                if keep is None:
                    products[q, j, at : at + count, :] = part
                else:
                    products[q, j, 0:8, :] = jnp.where(keep, part, 0.0)
                    products[q, j, rows + 8 : rows + 16, :] = jnp.where(keep, 0.0, part)

    def out_copy(slot):
        d, s = lax.div(slot, per_date), lax.rem(slot, per_date)
        return pltpu.make_async_copy(result.at[slot], out_ref.at[d, s], out_sem.at[slot])

    def one_slot(slot, carry):
        d, s = lax.div(slot, per_date), lax.rem(slot, per_date)
        used = s < count_ref[d]

        @pl.when(used)
        def _():
            v = lax.rem(partner_ref[d, s] - first_date + total_dates, total_dates)
            half = width_ref[d, s]
            write_products(0, 8, ends[d, 0], ends[d, 1], ends[v, 0], ends[v, 1], row == 1)
            for r in range(0, rows, 16):
                write_products(
                    8 + r, 16,
                    *(
                        held[lax.div(x, dates), lax.rem(x, dates), c, r : r + 16, :].astype(jnp.float32)
                        for x in (d, v)
                        for c in range(2)
                    ),
                )
            for q in range(4):
                for r in range(0, rows, 16):
                    for j in range(col_tiles):
                        taken = [products[q, j, r + 6 + k : r + 22 + k, :] for k in range(5)]
                        total = (taken[0] + taken[1]) + (taken[2] + taken[3]) + taken[4]
                        high = total.astype(jnp.bfloat16)
                        low = (total - high.astype(jnp.float32)).astype(jnp.bfloat16)
                        at = side + j * LANES
                        split[0, q * rows + r : q * rows + r + 16, at : at + LANES] = high
                        split[1, q * rows + r : q * rows + r + 16, at : at + LANES] = low
            matrix = bands[half - HALVES[0]]
            for c in range(0, columns, BLOCK):
                window = jnp.concatenate(
                    [split[0, :, c : c + 2 * BLOCK], split[1, :, c : c + 2 * BLOCK]], axis=1
                )
                box = jnp.dot(window, matrix, preferred_element_type=jnp.float32)
                box_re, box_im, box_u, box_v = (box[q * rows : (q + 1) * rows] for q in range(4))
                value = jnp.sqrt(box_re * box_re + box_im * box_im) * lax.rsqrt(box_u * box_v)
                result[slot, :, c : c + BLOCK] = value.astype(jnp.bfloat16)

        @pl.when(jnp.logical_not(used))
        def _():
            result[slot] = jnp.zeros((rows, columns), jnp.bfloat16)

        out_copy(slot).start()
        return carry

    lax.fori_loop(0, slots, one_slot, 0)
    for slot in range(slots):
        out_copy(slot).wait()


def coherence(partners, counts, windows, got, edge, reach, total_dates):
    blocks, dates, parts, rows, columns = got.shape
    per_date = partners.shape[1]
    held = dates * (reach + 1)
    anywhere = pl.BlockSpec(memory_space=pl.ANY)
    return pl.pallas_call(
        functools.partial(coherence_kernel, reach, total_dates),
        out_shape=jax.ShapeDtypeStruct((dates, per_date, rows, columns), jnp.bfloat16),
        in_specs=[pl.BlockSpec(memory_space=pltpu.HBM)] * 3 + [pl.BlockSpec(memory_space=pltpu.VMEM)] * 2,
        out_specs=anywhere,
        scratch_shapes=[
            pltpu.VMEM((held, parts, 8, columns), jnp.float32),
            pltpu.VMEM((4, columns // LANES, rows + 16, LANES), jnp.float32),
            pltpu.VMEM((len(HALVES), 4 * BLOCK, BLOCK), jnp.bfloat16),
            pltpu.VMEM((2, 4 * rows, columns + BLOCK), jnp.bfloat16),
            pltpu.VMEM((dates * per_date, rows, columns), jnp.bfloat16),
            pltpu.SMEM(partners.shape, jnp.int32),
            pltpu.SMEM(counts.shape, jnp.int32),
            pltpu.SMEM(windows.shape, jnp.int32),
            pltpu.SemaphoreType.DMA((3,)),
            pltpu.SemaphoreType.DMA((dates * per_date,)),
        ],
        compiler_params=pltpu.CompilerParams(vmem_limit_bytes=40 << 20),
        name="coherence",
    )(partners, counts, windows, got, edge)


def local(slc_stack, partners, counts, windows):
    dates = slc_stack.shape[0]
    loop_size = lax.axis_size("date")
    reach = loop_size // 4
    total_dates = dates * loop_size
    got, edge = exchange(slc_stack, loop_size, reach)
    return coherence(partners, counts, windows, got, edge, reach, total_dates)


def solution(mesh):
    in_specs = (
        P("date", None, ("tiles", "row"), None),
        P("date", None),
        P("date"),
        P("date", None),
    )
    out_specs = P("date", None, ("tiles", "row"), None)
    return jax.shard_map(local, mesh=mesh, in_specs=in_specs, out_specs=out_specs, check_vma=False)
```

```python
import functools
import jax
import jax.numpy as jnp
from jax import lax
from jax.experimental import pallas as pl
from jax.experimental.pallas import tpu as pltpu
from jax.sharding import PartitionSpec as P

MESH = pl.DeviceIdType.MESH
LANES = 128
PIECE = 32
BLOCK = 256
HALVES = (3, 4, 5)


def exchange_kernel(loop_size, reach, slc_ref, got_ref, edge_ref, rim, pack, *sems):
    rim_sem, own_sem, direct_send, direct_recv, near_send, near_recv, edge_send, edge_recv = sems
    dates, parts, rows, columns = slc_ref.shape
    tile = lax.axis_index("tiles")
    me = lax.axis_index("date")
    row = lax.axis_index("row")
    pieces = [
        (d, c, pl.ds(r, PIECE)) for d in range(dates) for c in range(parts) for r in range(0, rows, PIECE)
    ]
    relayed = reach == 2

    def at(steps, other=False):
        there = lax.rem(me + steps + loop_size, loop_size)
        return (tile, there, 1 - row if other else row)

    barrier = pltpu.get_barrier_semaphore()

    def greet(device):
        pl.semaphore_signal(barrier, inc=1, device_id=device, device_id_type=MESH)

    even = lax.rem(me, 2) == 0
    for k in range(reach + 1):
        greet(at(k, other=True))
    if relayed:
        greet(at(2))
        greet(at(jnp.where(even, 1, -1)))
    else:
        for k in range(1, reach + 1):
            greet(at(k))

    start = pl.multiple_of((1 - row) * (rows - 16), 16)
    rim_copy = pltpu.make_async_copy(slc_ref.at[:, :, pl.ds(start, 16), :], rim, rim_sem)
    rim_copy.start()
    rim_copy.wait()
    picked = []
    for d in range(dates):
        for c in range(parts):
            near_rows = rim[d, c].astype(jnp.float32)
            picked.append(jnp.where(row == 0, near_rows[14:16], near_rows[0:2]))
    spare = pack.shape[0] - 2 * len(picked)
    if spare:
        picked.append(jnp.zeros((spare, columns), jnp.float32))
    pack[...] = jnp.concatenate(picked, axis=0).astype(jnp.bfloat16)

    pl.semaphore_wait(barrier, 2 * reach + 1)

    def far(k, n):
        d, c, r = pieces[n]
        return pltpu.make_async_remote_copy(
            src_ref=slc_ref.at[d, c, r],
            dst_ref=got_ref.at[k, d, c, r],
            send_sem=direct_send.at[k - 1, n],
            recv_sem=direct_recv.at[k - 1, n],
            device_id=at(-k),
            device_id_type=MESH,
        )

    def near(n, src, steps):
        d, c, r = pieces[n]
        return pltpu.make_async_remote_copy(
            src_ref=src.at[d, c, r],
            dst_ref=got_ref.at[1, d, c, r],
            send_sem=near_send.at[n],
            recv_sem=near_recv.at[n],
            device_id=at(steps),
            device_id_type=MESH,
        )

    def edge(k):
        return pltpu.make_async_remote_copy(
            src_ref=pack,
            dst_ref=edge_ref.at[k],
            send_sem=edge_send.at[k],
            recv_sem=edge_recv.at[k],
            device_id=at(-k, other=True),
            device_id_type=MESH,
        )

    total = range(len(pieces))
    edges = [edge(k) for k in range(reach + 1)]
    own_copy = pltpu.make_async_copy(slc_ref, got_ref.at[0], own_sem)
    if relayed:
        for n in total:
            far(2, n).start()
            if n == 0:
                for e in edges:
                    e.start()

        own_copy.start()

        @pl.when(even)
        def _():
            for n in total:
                far(2, n).wait_recv()
                near(n, got_ref.at[2], 1).start()
            for n in total:
                near(n, got_ref.at[2], 1).wait()

        @pl.when(jnp.logical_not(even))
        def _():
            for n in total:
                near(n, slc_ref, -1).start()
            for n in total:
                far(2, n).wait_recv()
            for n in total:
                near(n, slc_ref, -1).wait()

        for n in total:
            far(2, n).wait_send()
    else:
        own_copy.start()
        for e in edges:
            e.start()
        for n in total:
            for k in range(1, reach + 1):
                far(k, n).start()
        for n in total:
            for k in range(1, reach + 1):
                far(k, n).wait()
    for e in edges:
        e.wait()
    own_copy.wait()


def exchange(slc, loop_size, reach):
    dates, parts, rows, columns = slc.shape
    pieces = dates * parts * (rows // PIECE)
    packed = -(-2 * dates * parts // 16) * 16
    return pl.pallas_call(
        functools.partial(exchange_kernel, loop_size, reach),
        out_shape=(
            jax.ShapeDtypeStruct((reach + 1,) + slc.shape, jnp.bfloat16),
            jax.ShapeDtypeStruct((reach + 1, packed, columns), jnp.bfloat16),
        ),
        in_specs=[pl.BlockSpec(memory_space=pltpu.HBM)],
        out_specs=(pl.BlockSpec(memory_space=pl.ANY), pl.BlockSpec(memory_space=pl.ANY)),
        scratch_shapes=[
            pltpu.VMEM((dates, parts, 16, columns), jnp.bfloat16),
            pltpu.VMEM((packed, columns), jnp.bfloat16),
            pltpu.SemaphoreType.DMA,
            pltpu.SemaphoreType.DMA,
            pltpu.SemaphoreType.DMA((reach, pieces)),
            pltpu.SemaphoreType.DMA((reach, pieces)),
            pltpu.SemaphoreType.DMA((pieces,)),
            pltpu.SemaphoreType.DMA((pieces,)),
            pltpu.SemaphoreType.DMA((reach + 1,)),
            pltpu.SemaphoreType.DMA((reach + 1,)),
        ],
        compiler_params=pltpu.CompilerParams(
            collective_id=0, has_side_effects=True, vmem_limit_bytes=16 << 20
        ),
        name="exchange",
    )(slc)


def band(half, block):
    def weights(into, out):
        return jnp.where(jnp.abs(into - out) <= half, 1.0, 0.0).astype(jnp.bfloat16)

    into = lax.broadcasted_iota(jnp.int32, (block, block), 0)
    out = lax.broadcasted_iota(jnp.int32, (block, block), 1)
    lane = into[:LANES]
    beside = jnp.where(lane < LANES // 2, block + lane, lane - LANES)
    return weights(into, out), weights(beside, out[:LANES])


def coherence_kernel(
    reach, total_dates, partner_ref, count_ref, width_ref, held, edges,
    out_ref, ends, products, bands, split, result,
    out_sem,
):
    blocks, dates, parts, rows, columns = held.shape
    per_date = out_ref.shape[1]
    col_tiles = columns // LANES
    slots = dates * per_date
    first_date = lax.axis_index("date") * dates
    row = lax.axis_index("row")
    for half in HALVES:
        middle, outer = band(half, BLOCK)
        for n, part in enumerate((middle, middle, outer, outer)):
            at = (n * BLOCK) if n < 2 else (2 * BLOCK + (n - 2) * LANES)
            bands[half - HALVES[0], at : at + part.shape[0], :] = part
    side = BLOCK // 2
    zeros = jnp.zeros((2, 4 * rows, side), jnp.bfloat16)
    split[:, :, 0:side] = zeros
    split[:, :, side + columns : 2 * side + columns] = zeros

    for k in range(reach + 1):
        block = edges[k].astype(jnp.float32)
        for d in range(dates):
            for c in range(parts):
                at = (d * parts + c) * 2
                ends[k * dates + d, c, 0:2, :] = block[at : at + 2]
                ends[k * dates + d, c, 6:8, :] = block[at : at + 2]

    def write_products(at, count, u_re, u_im, v_re, v_im, keep=None):
        values = (
            u_re * v_re + u_im * v_im,
            u_im * v_re - u_re * v_im,
            u_re * u_re + u_im * u_im,
            v_re * v_re + v_im * v_im,
        )
        for q, value in enumerate(values):
            for j in range(col_tiles):
                part = value[:, j * LANES : (j + 1) * LANES]
                if keep is None:
                    products[q, j, at : at + count, :] = part
                else:
                    products[q, j, 0:8, :] = jnp.where(keep, part, 0.0)
                    products[q, j, rows + 8 : rows + 16, :] = jnp.where(keep, 0.0, part)

    def out_copy(slot):
        d, s = lax.div(slot, per_date), lax.rem(slot, per_date)
        return pltpu.make_async_copy(result.at[slot], out_ref.at[d, s], out_sem.at[slot])

    def one_slot(slot, carry):
        d, s = lax.div(slot, per_date), lax.rem(slot, per_date)
        used = s < count_ref[d]

        @pl.when(used)
        def _():
            v = lax.rem(partner_ref[d, s] - first_date + total_dates, total_dates)
            half = width_ref[d, s]
            write_products(0, 8, ends[d, 0], ends[d, 1], ends[v, 0], ends[v, 1], row == 1)
            for r in range(0, rows, 16):
                write_products(
                    8 + r, 16,
                    *(
                        held[lax.div(x, dates), lax.rem(x, dates), c, r : r + 16, :].astype(jnp.float32)
                        for x in (d, v)
                        for c in range(2)
                    ),
                )
            for q in range(4):
                for r in range(0, rows, 16):
                    for j in range(col_tiles):
                        taken = [products[q, j, r + 6 + k : r + 22 + k, :] for k in range(5)]
                        total = (taken[0] + taken[1]) + (taken[2] + taken[3]) + taken[4]
                        high = total.astype(jnp.bfloat16)
                        low = (total - high.astype(jnp.float32)).astype(jnp.bfloat16)
                        at = side + j * LANES
                        split[0, q * rows + r : q * rows + r + 16, at : at + LANES] = high
                        split[1, q * rows + r : q * rows + r + 16, at : at + LANES] = low
            matrix = bands[half - HALVES[0]]
            lane = lax.broadcasted_iota(jnp.int32, (4 * rows, LANES), 1)
            for c in range(0, columns, BLOCK):
                middle = [split[n, :, side + c : side + c + BLOCK] for n in range(2)]
                outer = [
                    jnp.where(
                        lane < LANES // 2,
                        split[n, :, side + c + BLOCK : side + c + BLOCK + LANES],
                        split[n, :, side + c - LANES : side + c],
                    )
                    for n in range(2)
                ]
                window = jnp.concatenate(middle + outer, axis=1)
                box = jnp.dot(window, matrix, preferred_element_type=jnp.float32)
                box_re, box_im, box_u, box_v = (box[q * rows : (q + 1) * rows] for q in range(4))
                value = jnp.sqrt(box_re * box_re + box_im * box_im) * lax.rsqrt(box_u * box_v)
                result[slot, :, c : c + BLOCK] = value.astype(jnp.bfloat16)

        @pl.when(jnp.logical_not(used))
        def _():
            result[slot] = jnp.zeros((rows, columns), jnp.bfloat16)

        out_copy(slot).start()
        return carry

    lax.fori_loop(0, slots, one_slot, 0)
    for slot in range(slots):
        out_copy(slot).wait()


def coherence(partners, counts, windows, got, edge, reach, total_dates):
    blocks, dates, parts, rows, columns = got.shape
    per_date = partners.shape[1]
    held = dates * (reach + 1)
    anywhere = pl.BlockSpec(memory_space=pl.ANY)
    return pl.pallas_call(
        functools.partial(coherence_kernel, reach, total_dates),
        out_shape=jax.ShapeDtypeStruct((dates, per_date, rows, columns), jnp.bfloat16),
        in_specs=[pl.BlockSpec(memory_space=pltpu.SMEM)] * 3 + [pl.BlockSpec(memory_space=pltpu.VMEM)] * 2,
        out_specs=anywhere,
        scratch_shapes=[
            pltpu.VMEM((held, parts, 8, columns), jnp.float32),
            pltpu.VMEM((4, columns // LANES, rows + 16, LANES), jnp.float32),
            pltpu.VMEM((len(HALVES), 3 * BLOCK, BLOCK), jnp.bfloat16),
            pltpu.VMEM((2, 4 * rows, columns + BLOCK), jnp.bfloat16),
            pltpu.VMEM((dates * per_date, rows, columns), jnp.bfloat16),
            pltpu.SemaphoreType.DMA((dates * per_date,)),
        ],
        compiler_params=pltpu.CompilerParams(vmem_limit_bytes=40 << 20),
        name="coherence",
    )(partners, counts, windows, got, edge)


def local(slc_stack, partners, counts, windows):
    dates = slc_stack.shape[0]
    loop_size = lax.axis_size("date")
    reach = loop_size // 4
    total_dates = dates * loop_size
    got, edge = exchange(slc_stack, loop_size, reach)
    return coherence(partners, counts, windows, got, edge, reach, total_dates)


def solution(mesh):
    in_specs = (
        P("date", None, ("tiles", "row"), None),
        P("date", None),
        P("date"),
        P("date", None),
    )
    out_specs = P("date", None, ("tiles", "row"), None)
    return jax.shard_map(local, mesh=mesh, in_specs=in_specs, out_specs=out_specs, check_vma=False)
```
